256 devices in a mesh: grp: 16 (over x, y), help: 16 (over z, core).
Axes of the slice: x: 4, y: 4, z: 8, core: 2. Of those that a mesh axis runs over, the one named last changes fastest.
Arguments:
- embeddings: bfloat16 [131072, 768], P(('grp', 'help')), may hold values from -60 to 60, as said below
- cluster_ids: int32 [131072], P(('grp', 'help')), may hold values from 0 to 63, never falling along the last dimension, each value on 1 to 4096 neighbouring positions
- row_order: int32 [131072], P(('grp', 'help')), may hold values from 0 to 131071, each once
Outputs:
- best_match: float32 [131072], P(('grp', 'help'))
The draws below stay inside these ranges and needn't reach their ends.
Inputs may be any that keep to these rules, and one draw needn't show every extreme that they name: `cluster_ids`: never falls along the rows; every cluster holds 1 to 4096 consecutive rows, one exactly 4096. `row_order`: each value once. `embeddings`: rows have widely different scales.
All inputs are finite; a program needn't handle non-finite values.
Results may differ from the reference program's by a relative error of at most 0.0006.
Values may be sent and summed in bfloat16 or wider, within the bound.
No kernel may reach another device: no remote copies, remote signals or barrier semaphores. Data moves between devices by JAX's collectives and lax.ppermute only.
A program may use at most 128 MiB of HBM per device.

```python
import math
import jax
import jax.numpy as jnp
import numpy as np
from jax import lax

D = 768
ROWS = 131072
MAXC = 4096
CLUSTERS = 64


def draw_embeddings(key, part):
    key = jax.random.fold_in(key, 11)
    keys = jax.random.split(key, 8)
    bits = int(MAXC).bit_length() - 1
    scales = jnp.exp(jax.random.uniform(keys[0], (ROWS, 1), jnp.float32, 0.0, math.log(10.0)))
    base = jnp.clip(jax.random.normal(keys[1], (ROWS, D), jnp.float32), -6.0, 6.0)
    fresh = jnp.clip(jax.random.normal(keys[3], (ROWS, D), jnp.float32), -6.0, 6.0)
    level = jax.random.randint(keys[4], (ROWS,), 0, bits + 1)
    limit = jnp.left_shift(jnp.ones((ROWS,), jnp.int32), level)
    reach = 1 + jax.random.randint(keys[5], (ROWS,), jnp.zeros((ROWS,), jnp.int32), limit)
    partner = (jnp.arange(ROWS, dtype=jnp.int32) - reach) % ROWS
    copied = base[partner]
    noise_level = jnp.exp(jax.random.uniform(keys[6], (ROWS, 1), jnp.float32, math.log(0.03), 0.0))
    duplicate = (copied + noise_level * fresh) / (1.0 + noise_level)
    chosen = jax.random.randint(keys[7], (ROWS, 1), 0, 5) == 0
    values = jnp.where(chosen, duplicate, base) * scales
    return values.astype(jnp.bfloat16)


def profile(amount, total, most, slope):
    portions = [(1 << 20) // math.isqrt(rank ** slope) + 1 for rank in range(2, amount + 1)]
    rest, given = total - most - (amount - 1), [1] * (amount - 1)
    while rest > 0:
        candidates = [i for i in range(amount - 1) if given[i] < most]
        mass, budget = sum([portions[i] for i in candidates]), rest
        for i in candidates:
            more = min(most - given[i], max(1, budget * portions[i] // mass), rest)
            given[i] = given[i] + more
            rest = rest - more
    return np.array([most] + given)


def ragged(own_key, amount, total, bound, skew):
    if amount == 2:
        one = jax.random.randint(own_key, (), max(1, total - bound), min(bound, total - 1) + 1)
        return jnp.stack([one, total - one])
    tallies = jnp.asarray(profile(amount, total, bound, skew), jnp.int32)
    pairs = (amount - 1) // 2
    source_of, taker = tallies[1:1 + 2 * pairs:2], tallies[2:2 + 2 * pairs:2]
    margin = jnp.minimum(source_of - 1, bound - taker)
    shifted = jax.random.randint(jax.random.fold_in(own_key, 1), (pairs,), 0, 1 << 20) % (margin + 1)
    tallies = tallies.at[1:1 + 2 * pairs:2].set(source_of - shifted).at[2:2 + 2 * pairs:2].set(taker + shifted)
    return tallies[jax.random.permutation(jax.random.fold_in(own_key, 2), amount)]


def setup_inputs(seed: int = 0) -> dict:
    arg_keys = jax.random.split(jax.random.key(seed), 4)
    return {
        "embeddings": draw_embeddings(jax.random.fold_in(arg_keys[3], 71), 0),
        "cluster_ids": jnp.searchsorted(jnp.cumsum(ragged(arg_keys[1], CLUSTERS, ROWS, MAXC, 2)), jnp.arange(ROWS), side="right").astype(jnp.int32),
        "row_order": jax.random.permutation(arg_keys[2], ROWS).astype(jnp.int32),
    }


def reference(embeddings, cluster_ids, row_order):
    values = embeddings.astype(jnp.float32)
    scale = lax.rsqrt(lax.optimization_barrier(jnp.sum(values * values, axis=1, keepdims=True)) + 1e-06)
    unit = (values * scale).astype(jnp.bfloat16).astype(jnp.float32)
    block = min(512, ROWS)
    reach = MAXC
    pad_unit = jnp.pad(unit, ((reach, reach), (0, 0)))
    pad_ids = jnp.pad(cluster_ids, (reach, reach), constant_values=-1)
    pad_order = jnp.pad(row_order, (reach, reach))

    def one_block(index):
        start = (index * block).astype(jnp.int32)
        rows_unit = lax.dynamic_slice_in_dim(unit, start, block, 0)
        rows_ids = lax.dynamic_slice_in_dim(cluster_ids, start, block, 0)
        rows_order = lax.dynamic_slice_in_dim(row_order, start, block, 0)
        width = block + 2 * reach
        win_unit = lax.dynamic_slice_in_dim(pad_unit, start, width, 0)
        win_ids = lax.dynamic_slice_in_dim(pad_ids, start, width, 0)
        win_order = lax.dynamic_slice_in_dim(pad_order, start, width, 0)
        sims = jnp.dot(rows_unit, win_unit.T, precision=lax.Precision.HIGHEST, preferred_element_type=jnp.float32)
        valid = (rows_ids[:, None] == win_ids[None, :]) & (win_order[None, :] < rows_order[:, None])
        return lax.optimization_barrier(jnp.max(jnp.where(valid, sims, jnp.float32(-1.0)), axis=1))
    result = lax.map(one_block, jnp.arange(ROWS // block, dtype=jnp.int32))
    return result.reshape(ROWS)
```

```python
import functools
import jax
import jax.numpy as jnp
from jax import lax
from jax.experimental import pallas as pl
from jax.experimental.pallas import tpu as pltpu
from jax.sharding import PartitionSpec as P

AXES = ("grp", "help")
SPAN = 131072
EXTRA = 16
VMEM = 20 * 1024 * 1024


def pack_kernel(values_ref, labels_ref, order_ref, out_ref):
    rows, width = values_ref.shape
    values = values_ref[...].astype(jnp.float32)
    scale = lax.rsqrt(jnp.sum(values * values, axis=1, keepdims=True) + 1e-06)
    out_ref[:rows, :] = (values * scale).astype(jnp.bfloat16)
    key = (labels_ref[...] + 1) * SPAN + order_ref[...]
    line = lax.broadcasted_iota(jnp.int32, (EXTRA, rows), 0)
    digit = jnp.where(line == 0, key >> 16, jnp.where(line == 1, (key >> 8) & 255, key & 255))
    digit = jnp.where(line < 3, digit, 0)
    out_ref[rows:, :rows] = digit.astype(jnp.float32).astype(jnp.bfloat16)
    out_ref[rows:, rows:] = jnp.zeros((EXTRA, width - rows), jnp.bfloat16)


def pack(embeddings, cluster_ids, row_order):
    rows, width = embeddings.shape
    return pl.pallas_call(
        pack_kernel,
        out_shape=jax.ShapeDtypeStruct((rows + EXTRA, width), jnp.bfloat16),
        compiler_params=pltpu.CompilerParams(vmem_limit_bytes=VMEM),
    )(embeddings, cluster_ids.reshape(1, rows), row_order.reshape(1, rows))


def key_row(ref, rows):
    digits = ref[rows:, :rows].astype(jnp.float32)
    return digits[0:1] * 65536.0 + digits[1:2] * 256.0 + digits[2:3]


def best_kernel(plan, count, *refs):
    blocks, outs, columns = refs[:count], refs[count : count + len(plan)], refs[-1]
    rows = blocks[0].shape[0] - EXTRA
    keys = sorted({k for _, ks in plan for k in ks})
    for k in keys:
        columns[k] = jnp.broadcast_to(key_row(blocks[k], rows), (128, rows)).T
    for (q, ks), out in zip(plan, outs):
        row = key_row(blocks[q], rows)
        floor = ((row.astype(jnp.int32) >> 17) << 17).astype(jnp.float32)
        best = jnp.full((8, rows), -1.0, jnp.float32)
        for k in ks:
            sims = lax.dot_general(
                blocks[k][:rows, :], blocks[q][:rows, :], (((1,), (1,)), ((), ())),
                preferred_element_type=jnp.float32,
            )
            column = jnp.concatenate([columns[k]] * (rows // 128), axis=1)
            valid = (column < row) & (column >= floor)
            picked = jnp.where(valid, sims, -1.0)
            best = jnp.maximum(best, jnp.max(picked.reshape(rows // 8, 8, rows), axis=0))
        out[...] = jnp.max(best, axis=0, keepdims=True)


def best_of(blocks, plan, work=0):
    rows = blocks[0].shape[0] - EXTRA
    tiles = sum(len(ks) for _, ks in plan)
    return pl.pallas_call(
        functools.partial(best_kernel, plan, len(blocks)),
        out_shape=[jax.ShapeDtypeStruct((1, rows), jnp.float32) for _ in plan],
        scratch_shapes=[pltpu.VMEM((len(blocks), rows, 128), jnp.float32)],
        compiler_params=pltpu.CompilerParams(vmem_limit_bytes=VMEM),
        cost_estimate=pl.CostEstimate(flops=tiles + work, bytes_accessed=tiles, transcendentals=0),
    )(*blocks)


def keys_kernel(block_ref, out_ref):
    out_ref[...] = key_row(block_ref, out_ref.shape[1])


def keys_of(block):
    rows = block.shape[0] - EXTRA
    return pl.pallas_call(
        keys_kernel,
        out_shape=jax.ShapeDtypeStruct((1, rows), jnp.float32),
        compiler_params=pltpu.CompilerParams(vmem_limit_bytes=VMEM),
        cost_estimate=pl.CostEstimate(flops=10**9, bytes_accessed=1, transcendentals=0),
    )(block)


def move(x, even, odd):
    count = lax.axis_size(AXES)
    pairs = [(i, i + (odd if i % 2 else even)) for i in range(count)]
    return lax.ppermute(x, AXES, [(i, j) for i, j in pairs if 0 <= j < count])


def outward(x):
    return move(x, -2, 2)


def sibling(x):
    return move(x, 1, -1)


def message(x, even, odd):
    count, index = lax.axis_size(AXES), lax.axis_index(AXES)
    got = move(x, even, odd)
    if even % 2:
        even, odd = odd, even
    source = index - jnp.where(index % 2 == 0, even, odd)
    return jnp.where((source >= 0) & (source < count), got, -1.0)


def shards(embeddings, cluster_ids, row_order):
    own = pack(embeddings, cluster_ids, row_order)
    own_sib = sibling(own)
    near_a = outward(own)
    near_b = outward(own_sib)
    (best,) = best_of([own, own_sib], [(0, (0, 1))], 10**11)
    near_a, best = lax.optimization_barrier((near_a, best))
    far_a = outward(near_a)
    across_a = sibling(near_a)
    far_b = outward(near_b)
    across_b = sibling(near_b)
    near, near_sib = best_of([own, own_sib, near_a, near_b], [(0, (2, 3)), (1, (2, 3))])
    across2_a = sibling(far_a)
    far, far_sib, late = best_of(
        [own, own_sib, far_a, across_a, across_b], [(0, (2,)), (1, (2,)), (2, (3, 4))]
    )
    far_b, near, near_sib, far, far_sib, late = lax.optimization_barrier(
        (far_b, near, near_sib, far, far_sib, late)
    )
    best = jnp.maximum(jnp.maximum(best, near), far)
    best_sib = jnp.maximum(near_sib, far_sib)
    row = keys_of(far_b)
    across2_a, row = lax.optimization_barrier((across2_a, row))
    (opposite,) = best_of([across2_a, far_b], [(0, (1,))])
    opposite = sibling(opposite)
    far, far_sib, last, late2 = best_of(
        [own, own_sib, far_b, across_a, across_b, far_a, across2_a],
        [(0, (2,)), (1, (2,)), (2, (3, 4, 6)), (5, (6,))],
    )
    late = jnp.maximum(jnp.maximum(late, late2), jnp.where(row >= 0, opposite, -1.0))
    back = message(jnp.concatenate([late, last], axis=0), 4, -4)
    best = jnp.maximum(jnp.maximum(best, far), back[0:1])
    best_sib = jnp.maximum(jnp.maximum(best_sib, far_sib), back[1:2])
    return jnp.maximum(best, sibling(best_sib)).reshape(-1)


def solution(mesh):
    return jax.shard_map(
        shards,
        mesh=mesh,
        in_specs=(P(AXES, None), P(AXES), P(AXES)),
        out_specs=P(AXES),
        check_vma=False,
    )
```

```python
import functools
import jax
import jax.numpy as jnp
from jax import lax
from jax.experimental import pallas as pl
from jax.experimental.pallas import tpu as pltpu
from jax.sharding import PartitionSpec as P

AXES = ("grp", "help")
SPAN = 131072
EXTRA = 16
VMEM = 20 * 1024 * 1024


def pack_kernel(values_ref, labels_ref, order_ref, out_ref):
    rows, width = values_ref.shape
    values = values_ref[...].astype(jnp.float32)
    scale = lax.rsqrt(jnp.sum(values * values, axis=1, keepdims=True) + 1e-06)
    out_ref[:rows, :] = (values * scale).astype(jnp.bfloat16)
    key = (labels_ref[...] + 1) * SPAN + order_ref[...]
    line = lax.broadcasted_iota(jnp.int32, (EXTRA, rows), 0)
    digit = jnp.where(line == 0, key >> 16, jnp.where(line == 1, (key >> 8) & 255, key & 255))
    digit = jnp.where(line < 3, digit, 0)
    out_ref[rows:, :rows] = digit.astype(jnp.float32).astype(jnp.bfloat16)
    out_ref[rows:, rows:] = jnp.zeros((EXTRA, width - rows), jnp.bfloat16)


def pack(embeddings, cluster_ids, row_order):
    rows, width = embeddings.shape
    return pl.pallas_call(
        pack_kernel,
        out_shape=jax.ShapeDtypeStruct((rows + EXTRA, width), jnp.bfloat16),
        compiler_params=pltpu.CompilerParams(vmem_limit_bytes=VMEM),
    )(embeddings, cluster_ids.reshape(1, rows), row_order.reshape(1, rows))


def key_row(ref, rows):
    digits = ref[rows:, :rows].astype(jnp.float32)
    return digits[0:1] * 65536.0 + digits[1:2] * 256.0 + digits[2:3]


def best_kernel(plan, count, *refs):
    blocks, outs, columns = refs[:count], refs[count : count + len(plan)], refs[-1]
    rows = blocks[0].shape[0] - EXTRA
    keys = sorted({k for _, ks in plan for k in ks})
    for k in keys:
        columns[k] = jnp.broadcast_to(key_row(blocks[k], rows), (128, rows)).T
    for (q, ks), out in zip(plan, outs):
        row = key_row(blocks[q], rows)
        floor = ((row.astype(jnp.int32) >> 17) << 17).astype(jnp.float32)
        best = jnp.full((8, rows), -1.0, jnp.float32)
        for k in ks:
            sims = lax.dot_general(
                blocks[k][:rows, :], blocks[q][:rows, :], (((1,), (1,)), ((), ())),
                preferred_element_type=jnp.float32,
            )
            column = jnp.concatenate([columns[k]] * (rows // 128), axis=1)
            valid = (column < row) & (column >= floor)
            picked = jnp.where(valid, sims, -1.0)
            best = jnp.maximum(best, jnp.max(picked.reshape(rows // 8, 8, rows), axis=0))
        out[...] = jnp.max(best, axis=0, keepdims=True)


def best_of(blocks, plan, work=0):
    rows = blocks[0].shape[0] - EXTRA
    tiles = sum(len(ks) for _, ks in plan)
    return pl.pallas_call(
        functools.partial(best_kernel, plan, len(blocks)),
        out_shape=[jax.ShapeDtypeStruct((1, rows), jnp.float32) for _ in plan],
        scratch_shapes=[pltpu.VMEM((len(blocks), rows, 128), jnp.float32)],
        compiler_params=pltpu.CompilerParams(vmem_limit_bytes=VMEM),
        cost_estimate=pl.CostEstimate(flops=tiles + work, bytes_accessed=tiles, transcendentals=0),
    )(*blocks)


def keys_kernel(block_ref, out_ref):
    out_ref[...] = key_row(block_ref, out_ref.shape[1])


def keys_of(block):
    rows = block.shape[0] - EXTRA
    return pl.pallas_call(
        keys_kernel,
        out_shape=jax.ShapeDtypeStruct((1, rows), jnp.float32),
        compiler_params=pltpu.CompilerParams(vmem_limit_bytes=VMEM),
        cost_estimate=pl.CostEstimate(flops=10**9, bytes_accessed=1, transcendentals=0),
    )(block)


def along(x, step):
    count = lax.axis_size(AXES)
    ring = list(range(1, count, 2)) + list(range(count - 2, -1, -2))
    return lax.ppermute(x, AXES, [(ring[i], ring[(i + step) % count]) for i in range(count)])


def sibling(x):
    count = lax.axis_size(AXES)
    return lax.ppermute(x, AXES, [(i, i ^ 1) for i in range(count)])


def shards(embeddings, cluster_ids, row_order):
    own = pack(embeddings, cluster_ids, row_order)
    own_sib = sibling(own)
    near_a = along(own, 1)
    near_b = along(own_sib, 1)
    (best,) = best_of([own, own_sib], [(0, (0, 1))], 10**11)
    near_a, best = lax.optimization_barrier((near_a, best))
    far_a = along(near_a, 1)
    across_a = sibling(near_a)
    far_b = along(near_b, 1)
    across_b = sibling(near_b)
    near, near_sib = best_of([own, own_sib, near_a, near_b], [(0, (2, 3)), (1, (2, 3))])
    across2_a = sibling(far_a)
    far, far_sib, late = best_of(
        [own, own_sib, far_a, across_a, across_b], [(0, (2,)), (1, (2,)), (2, (3, 4))]
    )
    far_b, near, near_sib, far, far_sib, late = lax.optimization_barrier(
        (far_b, near, near_sib, far, far_sib, late)
    )
    best = jnp.maximum(jnp.maximum(best, near), far)
    best_sib = jnp.maximum(near_sib, far_sib)
    row = keys_of(far_b)
    across2_a, row = lax.optimization_barrier((across2_a, row))
    (opposite,) = best_of([across2_a, far_b], [(0, (1,))])
    opposite = sibling(opposite)
    last, late2 = best_of(
        [far_b, across_a, across_b, far_a, across2_a], [(0, (1, 2, 4)), (3, (4,))]
    )
    late = jnp.maximum(jnp.maximum(late, late2), jnp.where(row >= 0, opposite, -1.0))
    back = along(jnp.concatenate([late, last], axis=0), -2)
    far, far_sib = best_of([own, own_sib, far_b], [(0, (2,)), (1, (2,))], 10**10)
    best = jnp.maximum(jnp.maximum(best, far), back[0:1])
    best_sib = jnp.maximum(jnp.maximum(best_sib, far_sib), back[1:2])
    return jnp.maximum(best, sibling(best_sib)).reshape(-1)


def solution(mesh):
    return jax.shard_map(
        shards,
        mesh=mesh,
        in_specs=(P(AXES, None), P(AXES), P(AXES)),
        out_specs=P(AXES),
        check_vma=False,
    )
```

```python
import functools
import jax
import jax.numpy as jnp
from jax import lax
from jax.experimental import pallas as pl
from jax.experimental.pallas import tpu as pltpu
from jax.sharding import PartitionSpec as P

AXES = ("grp", "help")
SPAN = 131072
EXTRA = 16
VMEM = 20 * 1024 * 1024


def pack_kernel(count, *refs):
    for values_ref, key_ref, out_ref in zip(refs[:count], refs[count : 2 * count], refs[2 * count :]):
        rows, width = values_ref.shape
        values = values_ref[...].astype(jnp.float32)
        scale = lax.rsqrt(jnp.sum(values * values, axis=1, keepdims=True) + 1e-06)
        out_ref[:rows, :] = (values * scale).astype(jnp.bfloat16)
        key = key_ref[...]
        line = lax.broadcasted_iota(jnp.int32, (EXTRA, rows), 0)
        digit = jnp.where(line == 0, key >> 16, jnp.where(line == 1, (key >> 8) & 255, key & 255))
        digit = jnp.where(line < 3, digit, 0)
        out_ref[rows:, :rows] = digit.astype(jnp.float32).astype(jnp.bfloat16)
        out_ref[rows:, rows:] = jnp.zeros((EXTRA, width - rows), jnp.bfloat16)


def pack(values, keys):
    rows, width = values[0].shape
    return pl.pallas_call(
        functools.partial(pack_kernel, len(values)),
        out_shape=[jax.ShapeDtypeStruct((rows + EXTRA, width), jnp.bfloat16) for _ in values],
        compiler_params=pltpu.CompilerParams(vmem_limit_bytes=VMEM),
    )(*values, *keys)


def key_row(ref, rows):
    digits = ref[rows:, :rows].astype(jnp.float32)
    return digits[0:1] * 65536.0 + digits[1:2] * 256.0 + digits[2:3]


def best_kernel(plan, count, *refs):
    blocks, outs, columns = refs[:count], refs[count : count + len(plan)], refs[-1]
    rows = blocks[0].shape[0] - EXTRA
    keys = sorted({k for _, ks in plan for k in ks})
    for k in keys:
        columns[k] = jnp.broadcast_to(key_row(blocks[k], rows), (128, rows)).T
    for (q, ks), out in zip(plan, outs):
        row = key_row(blocks[q], rows)
        floor = ((row.astype(jnp.int32) >> 17) << 17).astype(jnp.float32)
        best = jnp.full((8, rows), -1.0, jnp.float32)
        for k in ks:
            sims = lax.dot_general(
                blocks[k][:rows, :], blocks[q][:rows, :], (((1,), (1,)), ((), ())),
                preferred_element_type=jnp.float32,
            )
            column = jnp.concatenate([columns[k]] * (rows // 128), axis=1)
            valid = (column < row) & (column >= floor)
            picked = jnp.where(valid, sims, -1.0)
            best = jnp.maximum(best, jnp.max(picked.reshape(rows // 8, 8, rows), axis=0))
        out[...] = jnp.max(best, axis=0, keepdims=True)


def best_of(blocks, plan, work=0):
    rows = blocks[0].shape[0] - EXTRA
    tiles = sum(len(ks) for _, ks in plan)
    return pl.pallas_call(
        functools.partial(best_kernel, plan, len(blocks)),
        out_shape=[jax.ShapeDtypeStruct((1, rows), jnp.float32) for _ in plan],
        scratch_shapes=[pltpu.VMEM((len(blocks), rows, 128), jnp.float32)],
        compiler_params=pltpu.CompilerParams(vmem_limit_bytes=VMEM),
        cost_estimate=pl.CostEstimate(flops=tiles + work, bytes_accessed=tiles, transcendentals=0),
    )(*blocks)


def keys_kernel(block_ref, out_ref):
    out_ref[...] = key_row(block_ref, out_ref.shape[1])


def keys_of(block):
    rows = block.shape[0] - EXTRA
    return pl.pallas_call(
        keys_kernel,
        out_shape=jax.ShapeDtypeStruct((1, rows), jnp.float32),
        compiler_params=pltpu.CompilerParams(vmem_limit_bytes=VMEM),
        cost_estimate=pl.CostEstimate(flops=10**9, bytes_accessed=1, transcendentals=0),
    )(block)


def along(x, step):
    count = lax.axis_size(AXES)
    ring = list(range(1, count, 2)) + list(range(count - 2, -1, -2))
    return lax.ppermute(x, AXES, [(ring[i], ring[(i + step) % count]) for i in range(count)])


def passed(x, work):
    return pl.pallas_call(
        lambda x_ref, out_ref: out_ref.__setitem__(..., x_ref[...]),
        out_shape=jax.ShapeDtypeStruct(x.shape, x.dtype),
        compiler_params=pltpu.CompilerParams(vmem_limit_bytes=VMEM),
        cost_estimate=pl.CostEstimate(flops=work, bytes_accessed=1, transcendentals=0),
    )(x)


def sibling(x):
    count = lax.axis_size(AXES)
    return lax.ppermute(x, AXES, [(i, i ^ 1) for i in range(count)])


def shards(embeddings, cluster_ids, row_order):
    near_raw = along(embeddings, 1)
    sib_raw = sibling(embeddings)
    key = ((cluster_ids + 1) * SPAN + row_order).reshape(1, -1)
    near_key = passed(along(key, 1), 10**9)
    own, own_sib = pack((embeddings, sib_raw), (key, sibling(key)))
    near_b = along(own_sib, 1)
    (best,) = best_of([own, own_sib], [(0, (0, 1))])
    (near_a,) = pack((near_raw,), (near_key,))
    far_a = along(near_a, 1)
    across_a = sibling(near_a)
    near_b, best = lax.optimization_barrier((near_b, best))
    far_b = along(near_b, 1)
    across_b = sibling(near_b)
    near, near_sib = best_of([own, own_sib, near_a, near_b], [(0, (2, 3)), (1, (2, 3))])
    across2_a = sibling(far_a)
    far, far_sib, late = best_of(
        [own, own_sib, far_a, across_a, across_b], [(0, (2,)), (1, (2,)), (2, (3, 4))]
    )
    far_b, near, near_sib, far, far_sib, late = lax.optimization_barrier(
        (far_b, near, near_sib, far, far_sib, late)
    )
    best = jnp.maximum(jnp.maximum(best, near), far)
    best_sib = jnp.maximum(near_sib, far_sib)
    row = keys_of(far_b)
    across2_a, row = lax.optimization_barrier((across2_a, row))
    (opposite,) = best_of([across2_a, far_b], [(0, (1,))])
    opposite = sibling(opposite)
    last, late2 = best_of(
        [far_b, across_a, across_b, far_a, across2_a], [(0, (1, 2, 4)), (3, (4,))]
    )
    late = jnp.maximum(jnp.maximum(late, late2), jnp.where(row >= 0, opposite, -1.0))
    back = along(jnp.concatenate([late, last], axis=0), -2)
    far, far_sib = best_of([own, own_sib, far_b], [(0, (2,)), (1, (2,))], 10**10)
    best = jnp.maximum(jnp.maximum(best, far), back[0:1])
    best_sib = jnp.maximum(jnp.maximum(best_sib, far_sib), back[1:2])
    return jnp.maximum(best, sibling(best_sib)).reshape(-1)


def solution(mesh):
    return jax.shard_map(
        shards,
        mesh=mesh,
        in_specs=(P(AXES, None), P(AXES), P(AXES)),
        out_specs=P(AXES),
        check_vma=False,
    )
```

```python
import functools
import jax
import jax.numpy as jnp
from jax import lax
from jax.experimental import pallas as pl
from jax.experimental.pallas import tpu as pltpu
from jax.sharding import PartitionSpec as P

AXES = ("grp", "help")
SPAN = 131072
EXTRA = 16
VMEM = 20 * 1024 * 1024


def pack_kernel(count, *refs):
    for values_ref, key_ref, out_ref in zip(refs[:count], refs[count : 2 * count], refs[2 * count :]):
        rows, width = values_ref.shape
        values = values_ref[...].astype(jnp.float32)
        scale = lax.rsqrt(jnp.sum(values * values, axis=1, keepdims=True) + 1e-06)
        out_ref[:rows, :] = (values * scale).astype(jnp.bfloat16)
        key = key_ref[...]
        line = lax.broadcasted_iota(jnp.int32, (EXTRA, rows), 0)
        digit = jnp.where(line == 0, key >> 16, jnp.where(line == 1, (key >> 8) & 255, key & 255))
        digit = jnp.where(line < 3, digit, 0)
        out_ref[rows:, :rows] = digit.astype(jnp.float32).astype(jnp.bfloat16)
        out_ref[rows:, rows:] = jnp.zeros((EXTRA, width - rows), jnp.bfloat16)


def pack(values, keys):
    rows, width = values[0].shape
    return pl.pallas_call(
        functools.partial(pack_kernel, len(values)),
        out_shape=[jax.ShapeDtypeStruct((rows + EXTRA, width), jnp.bfloat16) for _ in values],
        compiler_params=pltpu.CompilerParams(vmem_limit_bytes=VMEM),
    )(*values, *keys)


def key_row(ref, rows):
    digits = ref[rows:, :rows].astype(jnp.float32)
    return digits[0:1] * 65536.0 + digits[1:2] * 256.0 + digits[2:3]


def floor_of(key):
    return ((key.astype(jnp.int32) >> 17) << 17).astype(jnp.float32)


def best_kernel(plan, count, *refs):
    blocks, outs, columns = refs[:count], refs[count : count + len(plan)], refs[-1]
    rows = blocks[0].shape[0] - EXTRA
    keys = sorted({k for _, ks in plan for k in ks})
    for k in keys:
        columns[k] = jnp.broadcast_to(key_row(blocks[k], rows), (128, rows)).T
    for (q, ks), out in zip(plan, outs):
        row = key_row(blocks[q], rows)
        floor = floor_of(row)
        best = jnp.full((8, rows), -1.0, jnp.float32)
        for k in ks:
            sims = lax.dot_general(
                blocks[k][:rows, :], blocks[q][:rows, :], (((1,), (1,)), ((), ())),
                preferred_element_type=jnp.float32,
            )
            column = jnp.concatenate([columns[k]] * (rows // 128), axis=1)
            valid = (column < row) & (column >= floor)
            picked = jnp.where(valid, sims, -1.0)
            best = jnp.maximum(best, jnp.max(picked.reshape(rows // 8, 8, rows), axis=0))
        out[...] = jnp.max(best, axis=0, keepdims=True)


def pair_kernel(low_ref, high_ref, low_out, high_out):
    rows = low_ref.shape[0] - EXTRA
    sims = lax.dot_general(
        low_ref[:rows, :], high_ref[:rows, :], (((1,), (1,)), ((), ())),
        preferred_element_type=jnp.float32,
    )
    row, column = key_row(high_ref, rows), jnp.broadcast_to(key_row(low_ref, rows), (128, rows)).T
    row_floor, column_floor = floor_of(row), floor_of(column)
    best = jnp.full((rows, 128), -1.0, jnp.float32)
    for i in range(0, rows, 128):
        part = slice(i, i + 128)
        valid = (column < row[:, part]) & (column >= row_floor[:, part])
        picked = jnp.where(valid, sims[:, part], -1.0)
        high_out[:, part] = jnp.max(picked, axis=0, keepdims=True)
        valid = (row[:, part] < column) & (row[:, part] >= column_floor)
        best = jnp.maximum(best, jnp.where(valid, sims[:, part], -1.0))
    low_out[...] = jnp.max(best.T, axis=0, keepdims=True)


def best_of_pair(low, high):
    rows = low.shape[0] - EXTRA
    return pl.pallas_call(
        pair_kernel,
        out_shape=[jax.ShapeDtypeStruct((1, rows), jnp.float32)] * 2,
        compiler_params=pltpu.CompilerParams(vmem_limit_bytes=VMEM),
        cost_estimate=pl.CostEstimate(flops=1, bytes_accessed=1, transcendentals=0),
    )(low, high)


def best_of(blocks, plan, work=0):
    rows = blocks[0].shape[0] - EXTRA
    tiles = sum(len(ks) for _, ks in plan)
    return pl.pallas_call(
        functools.partial(best_kernel, plan, len(blocks)),
        out_shape=[jax.ShapeDtypeStruct((1, rows), jnp.float32) for _ in plan],
        scratch_shapes=[pltpu.VMEM((len(blocks), rows, 128), jnp.float32)],
        compiler_params=pltpu.CompilerParams(vmem_limit_bytes=VMEM),
        cost_estimate=pl.CostEstimate(flops=tiles + work, bytes_accessed=tiles, transcendentals=0),
    )(*blocks)


def along(x, step):
    count = lax.axis_size(AXES)
    ring = list(range(1, count, 2)) + list(range(count - 2, -1, -2))
    return lax.ppermute(x, AXES, [(ring[i], ring[(i + step) % count]) for i in range(count)])


def passed(x, work):
    return pl.pallas_call(
        lambda x_ref, out_ref: out_ref.__setitem__(..., x_ref[...]),
        out_shape=jax.ShapeDtypeStruct(x.shape, x.dtype),
        compiler_params=pltpu.CompilerParams(vmem_limit_bytes=VMEM),
        cost_estimate=pl.CostEstimate(flops=work, bytes_accessed=1, transcendentals=0),
    )(x)


def sibling(x):
    count = lax.axis_size(AXES)
    return lax.ppermute(x, AXES, [(i, i ^ 1) for i in range(count)])


def shards(embeddings, cluster_ids, row_order):
    near_raw = along(embeddings, 1)
    sib_raw = sibling(embeddings)
    key = ((cluster_ids + 1) * SPAN + row_order).reshape(1, -1)
    near_key = passed(along(key, 1), 3 * 10**9)
    own, own_sib = pack((embeddings, sib_raw), (key, sibling(key)))
    near_b = along(own_sib, 1)
    (best,) = best_of([own, own_sib], [(0, (0, 1))])
    (near_a,) = pack((near_raw,), (near_key,))
    far_a = along(near_a, 1)
    across_a = sibling(near_a)
    near_b, best = lax.optimization_barrier((near_b, best))
    far_b = along(near_b, 1)
    across_b = sibling(near_b)
    near, near_sib = best_of([own, own_sib, near_a, near_b], [(0, (2, 3)), (1, (2, 3))])
    across2_a = jnp.concatenate([sibling(far_a[0:272]), sibling(far_a[272:528])], axis=0)
    far, far_sib, late = best_of(
        [own, own_sib, far_a, across_a, across_b, across2_a], [(0, (2,)), (1, (2,)), (2, (3, 4, 5))]
    )
    far_b, near, near_sib, far, far_sib, late = lax.optimization_barrier(
        (far_b, near, near_sib, far, far_sib, late)
    )
    best = jnp.maximum(jnp.maximum(best, near), far)
    best_sib = jnp.maximum(near_sib, far_sib)
    last, opposite = best_of_pair(far_b, across2_a)
    opposite = sibling(opposite)
    (more,) = best_of([far_b, across_a, across_b], [(0, (1, 2))])
    late, last = jnp.maximum(late, opposite), jnp.maximum(last, more)
    back = along(jnp.concatenate([late, last], axis=0), -2)
    far, far_sib = best_of([own, own_sib, far_b], [(0, (2,)), (1, (2,))], 10**10)
    best = jnp.maximum(jnp.maximum(best, far), back[0:1])
    best_sib = jnp.maximum(jnp.maximum(best_sib, far_sib), back[1:2])
    return jnp.maximum(best, sibling(best_sib)).reshape(-1)


def solution(mesh):
    return jax.shard_map(
        shards,
        mesh=mesh,
        in_specs=(P(AXES, None), P(AXES), P(AXES)),
        out_specs=P(AXES),
        check_vma=False,
    )
```

```python
import functools
import jax
import jax.numpy as jnp
from jax import lax
from jax.experimental import pallas as pl
from jax.experimental.pallas import tpu as pltpu
from jax.sharding import PartitionSpec as P

AXES = ("grp", "help")
SPAN = 131072
EXTRA = 16
VMEM = 20 * 1024 * 1024


def pack_kernel(count, *refs):
    for values_ref, key_ref, out_ref in zip(refs[:count], refs[count : 2 * count], refs[2 * count :]):
        rows, width = values_ref.shape
        values = values_ref[...].astype(jnp.float32)
        scale = lax.rsqrt(jnp.sum(values * values, axis=1, keepdims=True) + 1e-06)
        out_ref[:rows, :] = (values * scale).astype(jnp.bfloat16)
        key = key_ref[...]
        line = lax.broadcasted_iota(jnp.int32, (EXTRA, rows), 0)
        digit = jnp.where(line == 0, key >> 16, jnp.where(line == 1, (key >> 8) & 255, key & 255))
        digit = jnp.where(line < 3, digit, 0)
        out_ref[rows:, :rows] = digit.astype(jnp.float32).astype(jnp.bfloat16)
        out_ref[rows:, rows:] = jnp.zeros((EXTRA, width - rows), jnp.bfloat16)


def pack(values, keys):
    rows, width = values[0].shape
    return pl.pallas_call(
        functools.partial(pack_kernel, len(values)),
        out_shape=[jax.ShapeDtypeStruct((rows + EXTRA, width), jnp.bfloat16) for _ in values],
        compiler_params=pltpu.CompilerParams(vmem_limit_bytes=VMEM),
    )(*values, *keys)


def key_row(ref, rows):
    digits = ref[rows:, :rows].astype(jnp.float32)
    return digits[0:1] * 65536.0 + digits[1:2] * 256.0 + digits[2:3]


def floor_of(key):
    return ((key.astype(jnp.int32) >> 17) << 17).astype(jnp.float32)


def best_kernel(plan, count, *refs):
    blocks, outs, columns = refs[:count], refs[count : count + len(plan)], refs[-1]
    rows = blocks[0].shape[0] - EXTRA
    keys = sorted({k for _, ks in plan for k in ks})
    for k in keys:
        columns[k] = jnp.broadcast_to(key_row(blocks[k], rows), (128, rows)).T
    for (q, ks), out in zip(plan, outs):
        row = key_row(blocks[q], rows)
        floor = floor_of(row)
        best = jnp.full((8, rows), -1.0, jnp.float32)
        for k in ks:
            sims = lax.dot_general(
                blocks[k][:rows, :], blocks[q][:rows, :], (((1,), (1,)), ((), ())),
                preferred_element_type=jnp.float32,
            )
            column = jnp.concatenate([columns[k]] * (rows // 128), axis=1)
            valid = (column < row) & (column >= floor)
            picked = jnp.where(valid, sims, -1.0)
            best = jnp.maximum(best, jnp.max(picked.reshape(rows // 8, 8, rows), axis=0))
        out[...] = jnp.max(best, axis=0, keepdims=True)


def pair_kernel(low_ref, high_ref, low_out, high_out):
    rows = low_ref.shape[0] - EXTRA
    sims = lax.dot_general(
        low_ref[:rows, :], high_ref[:rows, :], (((1,), (1,)), ((), ())),
        preferred_element_type=jnp.float32,
    )
    row, column = key_row(high_ref, rows), jnp.broadcast_to(key_row(low_ref, rows), (128, rows)).T
    row_floor, column_floor = floor_of(row), floor_of(column)
    best = jnp.full((rows, 128), -1.0, jnp.float32)
    for i in range(0, rows, 128):
        part = slice(i, i + 128)
        valid = (column < row[:, part]) & (column >= row_floor[:, part])
        picked = jnp.where(valid, sims[:, part], -1.0)
        high_out[:, part] = jnp.max(picked, axis=0, keepdims=True)
        valid = (row[:, part] < column) & (row[:, part] >= column_floor)
        best = jnp.maximum(best, jnp.where(valid, sims[:, part], -1.0))
    low_out[...] = jnp.max(best.T, axis=0, keepdims=True)


def best_of_pair(low, high):
    rows = low.shape[0] - EXTRA
    return pl.pallas_call(
        pair_kernel,
        out_shape=[jax.ShapeDtypeStruct((1, rows), jnp.float32)] * 2,
        compiler_params=pltpu.CompilerParams(vmem_limit_bytes=VMEM),
        cost_estimate=pl.CostEstimate(flops=1, bytes_accessed=1, transcendentals=0),
    )(low, high)


def best_of(blocks, plan, work=0):
    rows = blocks[0].shape[0] - EXTRA
    tiles = sum(len(ks) for _, ks in plan)
    return pl.pallas_call(
        functools.partial(best_kernel, plan, len(blocks)),
        out_shape=[jax.ShapeDtypeStruct((1, rows), jnp.float32) for _ in plan],
        scratch_shapes=[pltpu.VMEM((len(blocks), rows, 128), jnp.float32)],
        compiler_params=pltpu.CompilerParams(vmem_limit_bytes=VMEM),
        cost_estimate=pl.CostEstimate(flops=tiles + work, bytes_accessed=tiles, transcendentals=0),
    )(*blocks)


def along(x, step, other=0):
    count = lax.axis_size(AXES)
    ring = list(range(1, count, 2)) + list(range(count - 2, -1, -2))
    return lax.ppermute(x, AXES, [(ring[i], ring[(i + step) % count] ^ other) for i in range(count)])


def passed(x, work):
    return pl.pallas_call(
        lambda x_ref, out_ref: out_ref.__setitem__(..., x_ref[...]),
        out_shape=jax.ShapeDtypeStruct(x.shape, x.dtype),
        compiler_params=pltpu.CompilerParams(vmem_limit_bytes=VMEM),
        cost_estimate=pl.CostEstimate(flops=work, bytes_accessed=1, transcendentals=0),
    )(x)


def sibling(x):
    count = lax.axis_size(AXES)
    return lax.ppermute(x, AXES, [(i, i ^ 1) for i in range(count)])


def shards(embeddings, cluster_ids, row_order):
    near_raw = along(embeddings, 1)
    sib_raw = sibling(embeddings)
    key = ((cluster_ids + 1) * SPAN + row_order).reshape(1, -1)
    near_key = passed(along(key, 1), 3 * 10**9)
    own, own_sib = pack((embeddings, sib_raw), (key, sibling(key)))
    near_b = along(own_sib, 1)
    (best,) = best_of([own, own_sib], [(0, (0, 1))])
    (near_a,) = pack((near_raw,), (near_key,))
    far_a = along(near_a, 1)
    across_a = sibling(near_a)
    near_b, best = lax.optimization_barrier((near_b, best))
    far_b = along(near_b, 1)
    across_b = sibling(near_b)
    near, near_sib = best_of([own, own_sib, near_a, near_b], [(0, (2, 3)), (1, (2, 3))])
    across2_a = jnp.concatenate([sibling(far_a[0:272]), sibling(far_a[272:528])], axis=0)
    far, far_sib, late = best_of(
        [own, own_sib, far_a, across_a, across_b, across2_a], [(0, (2,)), (1, (2,)), (2, (3, 4, 5))]
    )
    far_b, near, near_sib, far, far_sib, late = lax.optimization_barrier(
        (far_b, near, near_sib, far, far_sib, late)
    )
    best = jnp.maximum(jnp.maximum(best, near), far)
    best_sib = jnp.maximum(near_sib, far_sib)
    last, opposite = best_of_pair(far_b, across2_a)
    opposite = sibling(opposite)
    (more,) = best_of([far_b, across_a, across_b], [(0, (1, 2))])
    late, last = jnp.maximum(late, opposite), jnp.maximum(last, more)
    back = along(jnp.concatenate([late, last], axis=0), -2, 1)
    far, far_sib = best_of([own, own_sib, far_b], [(0, (2,)), (1, (2,))], 10**10)
    best = jnp.maximum(jnp.maximum(best, far), back[1:2])
    best_sib = jnp.maximum(jnp.maximum(best_sib, far_sib), back[0:1])
    return jnp.maximum(best, sibling(best_sib)).reshape(-1)


def solution(mesh):
    return jax.shard_map(
        shards,
        mesh=mesh,
        in_specs=(P(AXES, None), P(AXES), P(AXES)),
        out_specs=P(AXES),
        check_vma=False,
    )
```

```python
import functools
import jax
import jax.numpy as jnp
from jax import lax
from jax.experimental import pallas as pl
from jax.experimental.pallas import tpu as pltpu
from jax.sharding import PartitionSpec as P

AXES = ("grp", "help")
SPAN = 131072
EXTRA = 16
VMEM = 20 * 1024 * 1024


def pack_kernel(count, *refs):
    for values_ref, key_ref, out_ref in zip(refs[:count], refs[count : 2 * count], refs[2 * count :]):
        rows, width = values_ref.shape
        values = values_ref[...].astype(jnp.float32)
        scale = lax.rsqrt(jnp.sum(values * values, axis=1, keepdims=True) + 1e-06)
        out_ref[:rows, :] = (values * scale).astype(jnp.bfloat16)
        key = key_ref[...]
        line = lax.broadcasted_iota(jnp.int32, (EXTRA, rows), 0)
        digit = jnp.where(line == 0, key >> 16, jnp.where(line == 1, (key >> 8) & 255, key & 255))
        digit = jnp.where(line < 3, digit, 0)
        out_ref[rows:, :rows] = digit.astype(jnp.float32).astype(jnp.bfloat16)
        out_ref[rows:, rows:] = jnp.zeros((EXTRA, width - rows), jnp.bfloat16)


def pack(values, keys):
    rows, width = values[0].shape
    return pl.pallas_call(
        functools.partial(pack_kernel, len(values)),
        out_shape=[jax.ShapeDtypeStruct((rows + EXTRA, width), jnp.bfloat16) for _ in values],
        compiler_params=pltpu.CompilerParams(vmem_limit_bytes=VMEM),
        cost_estimate=pl.CostEstimate(flops=1, bytes_accessed=1, transcendentals=0),
    )(*values, *keys)


def key_row(ref, rows):
    digits = ref[rows:, :rows].astype(jnp.float32)
    return digits[0:1] * 65536.0 + digits[1:2] * 256.0 + digits[2:3]


def floor_of(key):
    return ((key.astype(jnp.int32) >> 17) << 17).astype(jnp.float32)


def best_kernel(plan, count, *refs):
    blocks, outs, columns = refs[:count], refs[count : count + len(plan)], refs[-1]
    rows = blocks[0].shape[0] - EXTRA
    keys = sorted({k for _, ks in plan for k in ks})
    for k in keys:
        columns[k] = jnp.broadcast_to(key_row(blocks[k], rows), (128, rows)).T
    for (q, ks), out in zip(plan, outs):
        row = key_row(blocks[q], rows)
        floor = floor_of(row)
        best = jnp.full((8, rows), -1.0, jnp.float32)
        for k in ks:
            sims = lax.dot_general(
                blocks[k][:rows, :], blocks[q][:rows, :], (((1,), (1,)), ((), ())),
                preferred_element_type=jnp.float32,
            )
            column = jnp.concatenate([columns[k]] * (rows // 128), axis=1)
            valid = (column < row) & (column >= floor)
            picked = jnp.where(valid, sims, -1.0)
            best = jnp.maximum(best, jnp.max(picked.reshape(rows // 8, 8, rows), axis=0))
        out[...] = jnp.max(best, axis=0, keepdims=True)


def pair_kernel(low_ref, high_ref, low_out, high_out):
    rows = low_ref.shape[0] - EXTRA
    sims = lax.dot_general(
        low_ref[:rows, :], high_ref[:rows, :], (((1,), (1,)), ((), ())),
        preferred_element_type=jnp.float32,
    )
    row, column = key_row(high_ref, rows), jnp.broadcast_to(key_row(low_ref, rows), (128, rows)).T
    row_floor, column_floor = floor_of(row), floor_of(column)
    best = jnp.full((rows, 128), -1.0, jnp.float32)
    for i in range(0, rows, 128):
        part = slice(i, i + 128)
        valid = (column < row[:, part]) & (column >= row_floor[:, part])
        picked = jnp.where(valid, sims[:, part], -1.0)
        high_out[:, part] = jnp.max(picked, axis=0, keepdims=True)
        valid = (row[:, part] < column) & (row[:, part] >= column_floor)
        best = jnp.maximum(best, jnp.where(valid, sims[:, part], -1.0))
    low_out[...] = jnp.max(best.T, axis=0, keepdims=True)


def best_of_pair(low, high):
    rows = low.shape[0] - EXTRA
    return pl.pallas_call(
        pair_kernel,
        out_shape=[jax.ShapeDtypeStruct((1, rows), jnp.float32)] * 2,
        compiler_params=pltpu.CompilerParams(vmem_limit_bytes=VMEM),
        cost_estimate=pl.CostEstimate(flops=1, bytes_accessed=1, transcendentals=0),
    )(low, high)


def best_of(blocks, plan, work=0):
    rows = blocks[0].shape[0] - EXTRA
    tiles = sum(len(ks) for _, ks in plan)
    return pl.pallas_call(
        functools.partial(best_kernel, plan, len(blocks)),
        out_shape=[jax.ShapeDtypeStruct((1, rows), jnp.float32) for _ in plan],
        scratch_shapes=[pltpu.VMEM((len(blocks), rows, 128), jnp.float32)],
        compiler_params=pltpu.CompilerParams(vmem_limit_bytes=VMEM),
        cost_estimate=pl.CostEstimate(flops=tiles + work, bytes_accessed=tiles, transcendentals=0),
    )(*blocks)


def along(x, step, other=0):
    count = lax.axis_size(AXES)
    ring = list(range(1, count, 2)) + list(range(count - 2, -1, -2))
    return lax.ppermute(x, AXES, [(ring[i], ring[(i + step) % count] ^ other) for i in range(count)])


def passed(x, work):
    return pl.pallas_call(
        lambda x_ref, out_ref: out_ref.__setitem__(..., x_ref[...]),
        out_shape=jax.ShapeDtypeStruct(x.shape, x.dtype),
        compiler_params=pltpu.CompilerParams(vmem_limit_bytes=VMEM),
        cost_estimate=pl.CostEstimate(flops=work, bytes_accessed=1, transcendentals=0),
    )(x)


def sibling(x):
    count = lax.axis_size(AXES)
    return lax.ppermute(x, AXES, [(i, i ^ 1) for i in range(count)])


def shards(embeddings, cluster_ids, row_order):
    near_raw = along(embeddings, 1)
    sib_raw = sibling(embeddings)
    key = ((cluster_ids + 1) * SPAN + row_order).reshape(1, -1)
    near_key = passed(along(key, 1), 3 * 10**9)
    (own_sib,) = pack((sib_raw,), (sibling(key),))
    (own,) = pack((embeddings,), (key,))
    near_b = along(own_sib, 1)
    (best,) = best_of([own, own_sib], [(0, (0, 1))])
    (near_a,) = pack((near_raw,), (near_key,))
    far_a = along(near_a, 1)
    across_a = sibling(near_a)
    near_b, best = lax.optimization_barrier((near_b, best))
    far_b = along(near_b, 1)
    across_b = sibling(near_b)
    near, near_sib = best_of([own, own_sib, near_a, near_b], [(0, (2, 3)), (1, (2, 3))])
    across2_a = jnp.concatenate([sibling(far_a[0:272]), sibling(far_a[272:528])], axis=0)
    far, far_sib, late = best_of(
        [own, own_sib, far_a, across_a, across_b, across2_a], [(0, (2,)), (1, (2,)), (2, (3, 4, 5))]
    )
    far_b, near, near_sib, far, far_sib, late = lax.optimization_barrier(
        (far_b, near, near_sib, far, far_sib, late)
    )
    best = jnp.maximum(jnp.maximum(best, near), far)
    best_sib = jnp.maximum(near_sib, far_sib)
    last, opposite = best_of_pair(far_b, across2_a)
    opposite = sibling(opposite)
    (more,) = best_of([far_b, across_a, across_b], [(0, (1, 2))])
    late, last = jnp.maximum(late, opposite), jnp.maximum(last, more)
    message = jnp.concatenate([late, last], axis=0)
    back_sib, back = along(message, -2, 1), along(message, -2)
    own, own_sib, message = lax.optimization_barrier((own, own_sib, message))
    far, far_sib = best_of([own, own_sib, far_b], [(0, (2,)), (1, (2,))], 10**10)
    best = jnp.maximum(jnp.maximum(best, far), sibling(jnp.maximum(best_sib, far_sib)))
    return jnp.maximum(jnp.maximum(best, back[0:1]), back_sib[1:2]).reshape(-1)


def solution(mesh):
    return jax.shard_map(
        shards,
        mesh=mesh,
        in_specs=(P(AXES, None), P(AXES), P(AXES)),
        out_specs=P(AXES),
        check_vma=False,
    )
```

```python
import functools
import jax
import jax.numpy as jnp
from jax import lax
from jax.experimental import pallas as pl
from jax.experimental.pallas import tpu as pltpu
from jax.sharding import PartitionSpec as P

AXES = ("grp", "help")
SPAN = 131072
EXTRA = 16
VMEM = 20 * 1024 * 1024


def pack_kernel(count, *refs):
    for values_ref, key_ref, out_ref in zip(refs[:count], refs[count : 2 * count], refs[2 * count :]):
        rows, width = values_ref.shape
        values = values_ref[...].astype(jnp.float32)
        scale = lax.rsqrt(jnp.sum(values * values, axis=1, keepdims=True) + 1e-06)
        out_ref[:rows, :] = (values * scale).astype(jnp.bfloat16)
        key = key_ref[...]
        line = lax.broadcasted_iota(jnp.int32, (EXTRA, rows), 0)
        digit = jnp.where(line == 0, key >> 16, jnp.where(line == 1, (key >> 8) & 255, key & 255))
        digit = jnp.where(line < 3, digit, 0)
        out_ref[rows:, :rows] = digit.astype(jnp.float32).astype(jnp.bfloat16)
        out_ref[rows:, rows:] = jnp.zeros((EXTRA, width - rows), jnp.bfloat16)


def pack(values, keys):
    rows, width = values[0].shape
    return pl.pallas_call(
        functools.partial(pack_kernel, len(values)),
        out_shape=[jax.ShapeDtypeStruct((rows + EXTRA, width), jnp.bfloat16) for _ in values],
        compiler_params=pltpu.CompilerParams(vmem_limit_bytes=VMEM),
        cost_estimate=pl.CostEstimate(flops=1, bytes_accessed=1, transcendentals=0),
    )(*values, *keys)


def key_row(ref, rows):
    digits = ref[rows:, :rows].astype(jnp.float32)
    return digits[0:1] * 65536.0 + digits[1:2] * 256.0 + digits[2:3]


def floor_of(key):
    return ((key.astype(jnp.int32) >> 17) << 17).astype(jnp.float32)


def best_kernel(plan, count, *refs):
    blocks, outs, columns = refs[:count], refs[count : count + len(plan)], refs[-1]
    rows = blocks[0].shape[0] - EXTRA
    keys = sorted({k for _, ks in plan for k in ks})
    for k in keys:
        columns[k] = jnp.broadcast_to(key_row(blocks[k], rows), (128, rows)).T
    for (q, ks), out in zip(plan, outs):
        row = key_row(blocks[q], rows)
        floor = floor_of(row)
        best = jnp.full((8, rows), -1.0, jnp.float32)
        for k in ks:
            sims = lax.dot_general(
                blocks[k][:rows, :], blocks[q][:rows, :], (((1,), (1,)), ((), ())),
                preferred_element_type=jnp.float32,
            )
            column = jnp.concatenate([columns[k]] * (rows // 128), axis=1)
            valid = (column < row) & (column >= floor)
            picked = jnp.where(valid, sims, -1.0)
            best = jnp.maximum(best, jnp.max(picked.reshape(rows // 8, 8, rows), axis=0))
        out[...] = jnp.max(best, axis=0, keepdims=True)


def pair_kernel(low_ref, high_ref, low_out, high_out):
    rows = low_ref.shape[0] - EXTRA
    sims = lax.dot_general(
        low_ref[:rows, :], high_ref[:rows, :], (((1,), (1,)), ((), ())),
        preferred_element_type=jnp.float32,
    )
    row, column = key_row(high_ref, rows), jnp.broadcast_to(key_row(low_ref, rows), (128, rows)).T
    row_floor, column_floor = floor_of(row), floor_of(column)
    best = jnp.full((rows, 128), -1.0, jnp.float32)
    for i in range(0, rows, 128):
        part = slice(i, i + 128)
        valid = (column < row[:, part]) & (column >= row_floor[:, part])
        picked = jnp.where(valid, sims[:, part], -1.0)
        high_out[:, part] = jnp.max(picked, axis=0, keepdims=True)
        valid = (row[:, part] < column) & (row[:, part] >= column_floor)
        best = jnp.maximum(best, jnp.where(valid, sims[:, part], -1.0))
    low_out[...] = jnp.max(best.T, axis=0, keepdims=True)


def best_of_pair(low, high):
    rows = low.shape[0] - EXTRA
    return pl.pallas_call(
        pair_kernel,
        out_shape=[jax.ShapeDtypeStruct((1, rows), jnp.float32)] * 2,
        compiler_params=pltpu.CompilerParams(vmem_limit_bytes=VMEM),
        cost_estimate=pl.CostEstimate(flops=1, bytes_accessed=1, transcendentals=0),
    )(low, high)


def best_of(blocks, plan, work=0):
    rows = blocks[0].shape[0] - EXTRA
    tiles = sum(len(ks) for _, ks in plan)
    return pl.pallas_call(
        functools.partial(best_kernel, plan, len(blocks)),
        out_shape=[jax.ShapeDtypeStruct((1, rows), jnp.float32) for _ in plan],
        scratch_shapes=[pltpu.VMEM((len(blocks), rows, 128), jnp.float32)],
        compiler_params=pltpu.CompilerParams(vmem_limit_bytes=VMEM),
        cost_estimate=pl.CostEstimate(flops=tiles + work, bytes_accessed=tiles, transcendentals=0),
    )(*blocks)


def along(x, step, other=0):
    count = lax.axis_size(AXES)
    ring = list(range(1, count, 2)) + list(range(count - 2, -1, -2))
    return lax.ppermute(x, AXES, [(ring[i], ring[(i + step) % count] ^ other) for i in range(count)])


def passed(x, work):
    return pl.pallas_call(
        lambda x_ref, out_ref: out_ref.__setitem__(..., x_ref[...]),
        out_shape=jax.ShapeDtypeStruct(x.shape, x.dtype),
        compiler_params=pltpu.CompilerParams(vmem_limit_bytes=VMEM),
        cost_estimate=pl.CostEstimate(flops=work, bytes_accessed=1, transcendentals=0),
    )(x)


def sibling(x):
    count = lax.axis_size(AXES)
    return lax.ppermute(x, AXES, [(i, i ^ 1) for i in range(count)])


def shards(embeddings, cluster_ids, row_order):
    near_raw = along(embeddings, 1)
    sib_raw = sibling(embeddings)
    key = ((cluster_ids + 1) * SPAN + row_order).reshape(1, -1)
    near_key = passed(along(key, 1), 3 * 10**9)
    (own_sib,) = pack((sib_raw,), (sibling(key),))
    (own,) = pack((embeddings,), (key,))
    near_b = along(own_sib, 1)
    (best,) = best_of([own, own_sib], [(0, (0, 1))])
    (near_a,) = pack((near_raw,), (near_key,))
    far_a = along(near_a, 1)
    across_a = sibling(near_a)
    near_b, best = lax.optimization_barrier((near_b, best))
    far_b = along(near_b, 1)
    across_b = sibling(near_b)
    near, near_sib = best_of([own, own_sib, near_a, near_b], [(0, (2, 3)), (1, (2, 3))])
    across2_a = jnp.concatenate([sibling(far_a[0:272]), sibling(far_a[272:528])], axis=0)
    far, far_sib, late = best_of(
        [own, own_sib, far_a, across_a, across_b, across2_a], [(0, (2,)), (1, (2,)), (2, (3, 4, 5))]
    )
    far_b, near, near_sib, far, far_sib, late = lax.optimization_barrier(
        (far_b, near, near_sib, far, far_sib, late)
    )
    best = jnp.maximum(jnp.maximum(best, near), far)
    best_sib = jnp.maximum(near_sib, far_sib)
    last, opposite = best_of_pair(far_b, across2_a)
    opposite = sibling(opposite)
    (more,) = best_of([far_b, across_a, across_b], [(0, (1, 2))])
    late, last = jnp.maximum(late, opposite), jnp.maximum(last, more)
    back = along(jnp.concatenate([late, last], axis=0), -2, 1)
    far, far_sib = best_of([own, own_sib, far_b], [(0, (2,)), (1, (2,))], 10**10)
    best = jnp.maximum(jnp.maximum(best, far), back[1:2])
    best_sib = jnp.maximum(jnp.maximum(best_sib, far_sib), back[0:1])
    return jnp.maximum(best, sibling(best_sib)).reshape(-1)


def solution(mesh):
    return jax.shard_map(
        shards,
        mesh=mesh,
        in_specs=(P(AXES, None), P(AXES), P(AXES)),
        out_specs=P(AXES),
        check_vma=False,
    )
```

```python
import functools
import jax
import jax.numpy as jnp
from jax import lax
from jax.experimental import pallas as pl
from jax.experimental.pallas import tpu as pltpu
from jax.sharding import PartitionSpec as P

AXES = ("grp", "help")
SPAN = 131072
EXTRA = 16
VMEM = 20 * 1024 * 1024


def pack_kernel(count, *refs):
    for values_ref, key_ref, out_ref in zip(refs[:count], refs[count : 2 * count], refs[2 * count :]):
        rows, width = values_ref.shape
        values = values_ref[...].astype(jnp.float32)
        scale = lax.rsqrt(jnp.sum(values * values, axis=1, keepdims=True) + 1e-06)
        out_ref[:rows, :] = (values * scale).astype(jnp.bfloat16)
        key = key_ref[...]
        line = lax.broadcasted_iota(jnp.int32, (EXTRA, rows), 0)
        digit = jnp.where(line == 0, key >> 16, jnp.where(line == 1, (key >> 8) & 255, key & 255))
        digit = jnp.where(line < 3, digit, 0)
        out_ref[rows:, :rows] = digit.astype(jnp.float32).astype(jnp.bfloat16)
        out_ref[rows:, rows:] = jnp.zeros((EXTRA, width - rows), jnp.bfloat16)


def pack(values, keys):
    rows, width = values[0].shape
    return pl.pallas_call(
        functools.partial(pack_kernel, len(values)),
        out_shape=[jax.ShapeDtypeStruct((rows + EXTRA, width), jnp.bfloat16) for _ in values],
        compiler_params=pltpu.CompilerParams(vmem_limit_bytes=VMEM),
        cost_estimate=pl.CostEstimate(flops=1, bytes_accessed=1, transcendentals=0),
    )(*values, *keys)


def key_row(ref, rows):
    digits = ref[rows:, :rows].astype(jnp.float32)
    return digits[0:1] * 65536.0 + digits[1:2] * 256.0 + digits[2:3]


def floor_of(key):
    return ((key.astype(jnp.int32) >> 17) << 17).astype(jnp.float32)


def best_kernel(plan, count, *refs):
    blocks, outs, columns = refs[:count], refs[count : count + len(plan)], refs[-1]
    rows = blocks[0].shape[0] - EXTRA
    keys = sorted({k for _, ks in plan for k in ks})
    for k in keys:
        columns[k] = jnp.broadcast_to(key_row(blocks[k], rows), (128, rows)).T
    for (q, ks), out in zip(plan, outs):
        row = key_row(blocks[q], rows)
        floor = floor_of(row)
        best = jnp.full((8, rows), -1.0, jnp.float32)
        for k in ks:
            sims = lax.dot_general(
                blocks[k][:rows, :], blocks[q][:rows, :], (((1,), (1,)), ((), ())),
                preferred_element_type=jnp.float32,
            )
            column = jnp.concatenate([columns[k]] * (rows // 128), axis=1)
            valid = (column < row) & (column >= floor)
            picked = jnp.where(valid, sims, -1.0)
            best = jnp.maximum(best, jnp.max(picked.reshape(rows // 8, 8, rows), axis=0))
        out[...] = jnp.max(best, axis=0, keepdims=True)


def pair_kernel(low_ref, high_ref, low_out, high_out):
    rows = low_ref.shape[0] - EXTRA
    sims = lax.dot_general(
        low_ref[:rows, :], high_ref[:rows, :], (((1,), (1,)), ((), ())),
        preferred_element_type=jnp.float32,
    )
    row, column = key_row(high_ref, rows), jnp.broadcast_to(key_row(low_ref, rows), (128, rows)).T
    row_floor, column_floor = floor_of(row), floor_of(column)
    best = jnp.full((rows, 128), -1.0, jnp.float32)
    for i in range(0, rows, 128):
        part = slice(i, i + 128)
        valid = (column < row[:, part]) & (column >= row_floor[:, part])
        picked = jnp.where(valid, sims[:, part], -1.0)
        high_out[:, part] = jnp.max(picked, axis=0, keepdims=True)
        valid = (row[:, part] < column) & (row[:, part] >= column_floor)
        best = jnp.maximum(best, jnp.where(valid, sims[:, part], -1.0))
    low_out[...] = jnp.max(best.T, axis=0, keepdims=True)


def best_of_pair(low, high):
    rows = low.shape[0] - EXTRA
    return pl.pallas_call(
        pair_kernel,
        out_shape=[jax.ShapeDtypeStruct((1, rows), jnp.float32)] * 2,
        compiler_params=pltpu.CompilerParams(vmem_limit_bytes=VMEM),
        cost_estimate=pl.CostEstimate(flops=1, bytes_accessed=1, transcendentals=0),
    )(low, high)


def best_of(blocks, plan, work=0):
    rows = blocks[0].shape[0] - EXTRA
    tiles = sum(len(ks) for _, ks in plan)
    return pl.pallas_call(
        functools.partial(best_kernel, plan, len(blocks)),
        out_shape=[jax.ShapeDtypeStruct((1, rows), jnp.float32) for _ in plan],
        scratch_shapes=[pltpu.VMEM((len(blocks), rows, 128), jnp.float32)],
        compiler_params=pltpu.CompilerParams(vmem_limit_bytes=VMEM),
        cost_estimate=pl.CostEstimate(flops=tiles + work, bytes_accessed=tiles, transcendentals=0),
    )(*blocks)


def along(x, step, other=0):
    count = lax.axis_size(AXES)
    ring = list(range(1, count, 2)) + list(range(count - 2, -1, -2))
    return lax.ppermute(x, AXES, [(ring[i], ring[(i + step) % count] ^ other) for i in range(count)])


def passed(x, work):
    return pl.pallas_call(
        lambda x_ref, out_ref: out_ref.__setitem__(..., x_ref[...]),
        out_shape=jax.ShapeDtypeStruct(x.shape, x.dtype),
        compiler_params=pltpu.CompilerParams(vmem_limit_bytes=VMEM),
        cost_estimate=pl.CostEstimate(flops=work, bytes_accessed=1, transcendentals=0),
    )(x)


def sibling(x):
    count = lax.axis_size(AXES)
    return lax.ppermute(x, AXES, [(i, i ^ 1) for i in range(count)])


def shards(embeddings, cluster_ids, row_order):
    near_raw = along(embeddings, 1)
    sib_raw = sibling(embeddings)
    key = ((cluster_ids + 1) * SPAN + row_order).reshape(1, -1)
    near_key = passed(along(key, 1), 3 * 10**9)
    (own_sib,) = pack((sib_raw,), (sibling(key),))
    (own,) = pack((embeddings,), (key,))
    near_b = along(own_sib, 1)
    (best,) = best_of([own, own_sib], [(0, (0, 1))])
    (near_a,) = pack((near_raw,), (near_key,))
    far_a = along(near_a, 1)
    across_a = sibling(near_a)
    near_b, best = lax.optimization_barrier((near_b, best))
    far_b = along(near_b, 1)
    across_b = sibling(near_b)
    near, near_sib = best_of([own, own_sib, near_a, near_b], [(0, (2, 3)), (1, (2, 3))])
    across2_a = jnp.concatenate([sibling(far_a[0:272]), sibling(far_a[272:528])], axis=0)
    far, far_sib, late = best_of(
        [own, own_sib, far_a, across_a, across_b, across2_a], [(0, (2,)), (1, (2,)), (2, (3, 4, 5))]
    )
    far_b, near, near_sib, far, far_sib, late = lax.optimization_barrier(
        (far_b, near, near_sib, far, far_sib, late)
    )
    best = jnp.maximum(jnp.maximum(best, near), far)
    best_sib = jnp.maximum(near_sib, far_sib)
    last, opposite = best_of_pair(far_b, across2_a)
    opposite = sibling(opposite)
    (more,) = best_of([far_b, across_a, across_b], [(0, (1, 2))])
    late, last = jnp.maximum(late, opposite), jnp.maximum(last, more)
    message = jnp.concatenate([late, last], axis=0)
    back_sib, back = along(message, -2, 1), along(message, -2)
    own, own_sib, message = lax.optimization_barrier((own, own_sib, message))
    far, far_sib = best_of([own, own_sib, far_b], [(0, (2,)), (1, (2,))], 10**10)
    best = jnp.maximum(jnp.maximum(best, far), sibling(jnp.maximum(best_sib, far_sib)))
    return jnp.maximum(jnp.maximum(best, back_sib[1:2]), back[0:1]).reshape(-1)


def solution(mesh):
    return jax.shard_map(
        shards,
        mesh=mesh,
        in_specs=(P(AXES, None), P(AXES), P(AXES)),
        out_specs=P(AXES),
        check_vma=False,
    )
```
